512 devices in a mesh: dp: 64 (over z, y_lo, core), tensor: 8 (over x, y_hi).
Axes of the slice: x: 4, y: 8 (y_hi: 2, y_lo: 4; y = y_hi * 4 + y_lo), z: 8, core: 2. Of those that a mesh axis runs over, the one named last changes fastest.
Arguments:
- queries: bfloat16 [32768, 8192], P(('dp', 'tensor')), may hold values from -160 to 160
- key_rows: bfloat16 [32768, 1024], P(('dp', 'tensor')), may hold values from -6 to 6
- value_rows_initial: bfloat16 [32768, 1024], P(('dp', 'tensor')), may hold values from -6 to 6
- grad_out: bfloat16 [32768, 8192], P('dp', 'tensor'), may hold values from -6 to 6
- seg_ids: int32 [64, 512], replicated, may hold values from 0 to 8, as said below
- pair_mask: int32 [64], replicated, may hold values from 0 to 63, as said below
- sender: int32 [64], replicated, may hold values from 0 to 1, as said below
- moved_seq: int32 [64], replicated, may hold values from 0 to 7, as said below
Outputs:
- attn_out: bfloat16 [32768, 8192], P('dp', 'tensor')
- grad_queries: bfloat16 [32768, 8192], P(('dp', 'tensor'))
- grad_keys: bfloat16 [32768, 1024], P(('dp', 'tensor'))
- grad_values: bfloat16 [32768, 1024], P(('dp', 'tensor'))
The draws below stay inside these ranges and needn't reach their ends.
Inputs may be any that keep to these rules, and one draw needn't show every extreme that they name: `seg_ids`: each row is non-decreasing: every label 0 to 7 is used by a run of slots, then 8 fills the unused slots. `pair_mask`: entry g is g XOR m for one m of 1 to 63 common to all groups (so m is entry 0). `sender`: exactly one group of every pair has 1. A giving group's sequence moved_seq has at most 128 rows, exactly 128 for some group; a receiving group uses at most 384 slots, exactly that many for some group; some giving group uses all 512. `moved_seq`: read only for giving groups.
All inputs are finite; a program needn't handle non-finite values.
Results may differ from the reference program's by a relative error of at most 0.0091.
Values may be sent and summed in bfloat16 or wider, within the bound.
No kernel may reach another device: no remote copies, remote signals or barrier semaphores. Data moves between devices by JAX's collectives and lax.ppermute only.
A program may use at most 128 MiB of HBM per device.

```python
import jax
import jax.numpy as jnp
from jax import lax

QUERY_HEADS = 64
KEY_VALUE_HEADS = 8
HEAD_DIMENSION = 128
TOK_DEV = 512
SEQS = 8
MOVE = 128
TOTAL_ROW_SLOTS = 32768
N_DP = 64


def pair_layout(key):
    key = jax.random.fold_in(key, 101)
    parts = jax.random.split(key, 7)
    groups = jnp.arange(N_DP, dtype=jnp.int32)
    xor_value = jax.random.randint(parts[0], (), 1, N_DP, dtype=jnp.int32)
    partner = jnp.bitwise_xor(groups, xor_value)
    coin = jax.random.randint(parts[1], (N_DP,), 0, 2, dtype=jnp.int32)
    sender = jnp.where(groups < partner, coin, 1 - coin[partner])
    first_send = jnp.argmax(sender)
    first_recv = jnp.argmin(sender)
    moved = jax.random.randint(parts[2], (N_DP,), 0, SEQS, dtype=jnp.int32)
    moved_len = jax.random.randint(parts[3], (N_DP,), MOVE // 4, MOVE + 1, dtype=jnp.int32)
    moved_len = jnp.where(groups == first_send, MOVE, moved_len)
    live_send = jax.random.randint(parts[4], (N_DP,), TOK_DEV - MOVE // 2, TOK_DEV + 1, dtype=jnp.int32)
    live_send = jnp.where(groups == first_send, TOK_DEV, live_send)
    live_recv = jax.random.randint(parts[5], (N_DP,), TOK_DEV // 4, TOK_DEV - MOVE + 1, dtype=jnp.int32)
    live_recv = jnp.where(groups == first_recv, TOK_DEV - MOVE, live_recv)
    live = jnp.where(sender == 1, live_send, live_recv)
    shares = jax.random.randint(parts[6], (N_DP, SEQS), 1, 1000, dtype=jnp.int32)
    slots = jnp.arange(SEQS, dtype=jnp.int32)[None, :]
    is_moved = (slots == moved[:, None]) & (sender[:, None] == 1)
    shares = jnp.where(is_moved, 0, shares)
    free_parts = SEQS - sender
    rest = live - sender * moved_len - free_parts
    portion = rest[:, None] * shares // jnp.sum(shares, axis=1, keepdims=True)
    lengths = jnp.where(is_moved, moved_len[:, None], 1 + portion)
    target = jnp.where((sender == 1) & (moved == SEQS - 1), SEQS - 2, SEQS - 1)
    deficit = live - jnp.sum(lengths, axis=1)
    lengths = lengths + jnp.where(slots == target[:, None], deficit[:, None], 0)
    ends = jnp.cumsum(lengths, axis=1)
    rows = jnp.arange(TOK_DEV, dtype=jnp.int32)
    sequence_labels = jnp.sum((rows[None, :, None] >= ends[:, None, :]).astype(jnp.int32), axis=2)
    return (sequence_labels.astype(jnp.int32), partner.astype(jnp.int32), sender.astype(jnp.int32), moved)


def shared_keys(key):
    key = jax.random.fold_in(key, 202)
    return jnp.clip(jax.random.normal(key, (TOTAL_ROW_SLOTS, KEY_VALUE_HEADS * HEAD_DIMENSION), jnp.float32), -5.0, 5.0)


def draw_seg_ids(key, part):
    layout = pair_layout(key)
    return layout[0]


def draw_pair_mask(key, part):
    layout = pair_layout(key)
    return layout[1]


def draw_sender(key, part):
    layout = pair_layout(key)
    return layout[2]


def draw_moved_seq(key, part):
    layout = pair_layout(key)
    return layout[3]


def draw_queries(key, part):
    key = jax.random.fold_in(key, 3)
    fresh = jnp.clip(jax.random.normal(key, (TOTAL_ROW_SLOTS, QUERY_HEADS * HEAD_DIMENSION), jnp.float32), -6.0, 6.0)
    return fresh.astype(jnp.bfloat16)


def draw_key_rows(key, part):
    base_offset = shared_keys(key)
    return base_offset.astype(jnp.bfloat16)


def block_levels(rng, shape, cuts, low, high):
    def one(dim, shards_of):
        steps = jax.random.uniform(jax.random.fold_in(jax.random.fold_in(rng, 6), dim), (shards_of,), jnp.float32, low / len(cuts), high / len(cuts))
        return jnp.repeat(jnp.exp(steps), shape[dim] // shards_of).reshape((-1,) + (1,) * (len(shape) - dim - 1))

    level = one(*cuts[0])
    for cut in cuts[1:]:
        level = level * one(*cut)
    return level


def gaussian(stream_key, extent, width, reach, pieces=(), held_as=jnp.bfloat16):
    values = width * jax.random.normal(stream_key, extent, jnp.float32)
    if pieces:
        values = values * block_levels(stream_key, extent, pieces, -0.22, 0.18)
    return jnp.clip(values, -reach, reach).astype(held_as)


def setup_inputs(seed: int = 0) -> dict:
    splits = jax.random.split(jax.random.key(seed), 9)
    return {
        "queries": draw_queries(jax.random.fold_in(splits[8], 71), 0),
        "key_rows": draw_key_rows(jax.random.fold_in(splits[8], 71), 0),
        "value_rows_initial": gaussian(splits[2], (TOTAL_ROW_SLOTS, KEY_VALUE_HEADS * HEAD_DIMENSION), 1.0, 6.0, ((0, 512),)),
        "grad_out": gaussian(splits[3], (TOTAL_ROW_SLOTS, QUERY_HEADS * HEAD_DIMENSION), 1.0, 6.0, ((0, 64), (1, 8))),
        "seg_ids": draw_seg_ids(jax.random.fold_in(splits[8], 71), 0),
        "pair_mask": draw_pair_mask(jax.random.fold_in(splits[8], 71), 0),
        "sender": draw_sender(jax.random.fold_in(splits[8], 71), 0),
        "moved_seq": draw_moved_seq(jax.random.fold_in(splits[8], 71), 0),
    }


def head_pass(query_head, key_head, value_head, grad_head, allowed, live_rows, factor):
    scores = jnp.dot(query_head, key_head.T, preferred_element_type=jnp.float32) * factor
    scores = jnp.where(allowed, scores, jnp.float32(-1e30))
    row_peak = jnp.max(scores, axis=1, keepdims=True)
    weights = jnp.exp(scores - row_peak)
    softmax_rows = weights / jnp.sum(weights, axis=1, keepdims=True)
    probs_low = softmax_rows.astype(jnp.bfloat16)
    output = jnp.dot(probs_low, value_head, preferred_element_type=jnp.float32)
    output = jnp.where(live_rows[:, None], output, jnp.zeros_like(output)).astype(jnp.bfloat16)
    grad_live = jnp.where(live_rows[:, None], grad_head, jnp.zeros_like(grad_head))
    grad_value = jnp.dot(probs_low.T, grad_live, preferred_element_type=jnp.float32)
    grad_probs = jnp.dot(grad_live, value_head.T, preferred_element_type=jnp.float32)
    center = jnp.sum(grad_live.astype(jnp.float32) * output.astype(jnp.float32), axis=1, keepdims=True)
    grad_scores = (softmax_rows * (grad_probs - center)).astype(jnp.bfloat16)
    grad_query = (jnp.dot(grad_scores, key_head, preferred_element_type=jnp.float32) * factor).astype(jnp.bfloat16)
    grad_key = jnp.dot(grad_scores.T, query_head, preferred_element_type=jnp.float32) * factor
    return output, grad_query, grad_key, grad_value


def attend_block(updated_rows, sequence_labels, grad_rows, heads_q, heads_kv, head_size):
    count_rows = updated_rows.shape[0]
    query_cols = heads_q * head_size
    key_value_columns = heads_kv * head_size
    query_part = updated_rows[:, :query_cols].reshape(count_rows, heads_q, head_size).transpose(1, 0, 2)
    key_part = updated_rows[:, query_cols:query_cols + key_value_columns].reshape(count_rows, heads_kv, head_size).transpose(1, 0, 2)
    value_part = updated_rows[:, query_cols + key_value_columns:].reshape(count_rows, heads_kv, head_size).transpose(1, 0, 2)
    grad_part = grad_rows.reshape(count_rows, heads_q, head_size).transpose(1, 0, 2)
    positions = jnp.arange(count_rows, dtype=jnp.int32)
    live_rows = sequence_labels != SEQS
    allowed = ((sequence_labels[:, None] == sequence_labels[None, :]) & live_rows[:, None] & (positions[None, :] <= positions[:, None])) | (positions[:, None] == positions[None, :])
    group_size = heads_q // heads_kv
    factor = head_size ** -0.5

    def per_head(head_item):
        head_index, query_head, grad_head = head_item
        kv_index = head_index // group_size
        key_head = lax.dynamic_index_in_dim(key_part, kv_index, 0, keepdims=False)
        value_head = lax.dynamic_index_in_dim(value_part, kv_index, 0, keepdims=False)
        return head_pass(query_head, key_head, value_head, grad_head, allowed, live_rows, factor)

    outputs, grad_query, grad_key, grad_value = lax.map(per_head, (jnp.arange(heads_q, dtype=jnp.int32), query_part, grad_part))
    attention = outputs.transpose(1, 0, 2).reshape(count_rows, query_cols)
    grad_key = grad_key.reshape(heads_kv, group_size, count_rows, head_size).sum(axis=1).astype(jnp.bfloat16)
    grad_value = grad_value.reshape(heads_kv, group_size, count_rows, head_size).sum(axis=1).astype(jnp.bfloat16)
    gradients = jnp.concatenate([grad_query.transpose(1, 0, 2).reshape(count_rows, query_cols), grad_key.transpose(1, 0, 2).reshape(count_rows, key_value_columns), grad_value.transpose(1, 0, 2).reshape(count_rows, key_value_columns)], axis=1)
    return attention, gradients


def reference(queries, key_rows, value_rows_initial, grad_out, seg_ids, pair_mask, sender, moved_seq):
    query_cols = QUERY_HEADS * HEAD_DIMENSION
    key_value_columns = KEY_VALUE_HEADS * HEAD_DIMENSION
    row_width = query_cols + 2 * key_value_columns
    groups = jnp.arange(N_DP, dtype=jnp.int32)
    xor_value = pair_mask[0]
    partner = jnp.bitwise_xor(groups, xor_value)
    live_all = jnp.sum(seg_ids < SEQS, axis=1).astype(jnp.int32)
    start_all = jnp.sum(seg_ids < moved_seq[:, None], axis=1).astype(jnp.int32)
    count_all = jnp.sum(seg_ids == moved_seq[:, None], axis=1).astype(jnp.int32)
    rows_all = jnp.concatenate([queries, key_rows, value_rows_initial], axis=1).reshape(N_DP, TOK_DEV, row_width)
    padded = jnp.concatenate([rows_all, jnp.zeros((N_DP, MOVE, row_width), jnp.bfloat16)], axis=1)
    gradient_groups = grad_out.reshape(N_DP, TOK_DEV, query_cols)
    positions = jnp.arange(TOK_DEV, dtype=jnp.int32)

    def one_group(group_position_index):
        partner_index = partner[group_position_index]
        packet = lax.dynamic_slice_in_dim(padded[partner_index], start_all[partner_index], MOVE, 0)
        placed = lax.dynamic_update_slice_in_dim(padded[group_position_index], packet, live_all[group_position_index], 0)[:TOK_DEV]
        giving = sender[group_position_index] == 1
        own_labels = seg_ids[group_position_index]
        live_here = live_all[group_position_index]
        sequence_labels = jnp.where(giving, jnp.where(own_labels == moved_seq[group_position_index], SEQS, own_labels), jnp.where(positions < live_here, own_labels, jnp.where(positions < live_here + count_all[partner_index], SEQS + 1, SEQS)))
        updated_rows = jnp.where(giving, rows_all[group_position_index], placed)
        return attend_block(updated_rows, sequence_labels, gradient_groups[group_position_index], QUERY_HEADS, KEY_VALUE_HEADS, HEAD_DIMENSION)

    attention, gradients = lax.map(one_group, groups)
    grads_padded = jnp.concatenate([gradients, jnp.zeros((N_DP, MOVE, row_width), jnp.bfloat16)], axis=1)

    def restore(group_position_index):
        partner_index = partner[group_position_index]
        returning = lax.dynamic_slice_in_dim(grads_padded[partner_index], live_all[partner_index], MOVE, 0)
        back_placed = lax.dynamic_update_slice_in_dim(jnp.zeros((TOK_DEV + MOVE, row_width), jnp.bfloat16), returning, start_all[group_position_index], 0)[:TOK_DEV]
        giving = sender[group_position_index] == 1
        own_labels = seg_ids[group_position_index]
        own_grads = gradients[group_position_index]
        handed = jnp.where((own_labels == moved_seq[group_position_index])[:, None], back_placed, own_grads)
        kept = jnp.where((positions < live_all[group_position_index])[:, None], own_grads, jnp.zeros_like(own_grads))
        return jnp.where(giving, handed, kept)

    restored = lax.map(restore, groups).reshape(TOTAL_ROW_SLOTS, row_width)
    return (attention.reshape(TOTAL_ROW_SLOTS, query_cols), restored[:, :query_cols], restored[:, query_cols:query_cols + key_value_columns], restored[:, query_cols + key_value_columns:])
```

```python
import functools

import jax
import jax.numpy as jnp
from jax import lax
from jax.experimental import pallas as pl
from jax.experimental.pallas import tpu as pltpu
from jax.sharding import PartitionSpec as P

HEAD = 128
SEQS = 8
MOVE = 128
FACTOR = HEAD**-0.5
LOG2E = 1.4426950408889634
BLOCKED = -1e30


def dot(a, b, contract_a, contract_b):
    return lax.dot_general(
        a, b, (((contract_a,), (contract_b,)), ((), ())), preferred_element_type=jnp.float32
    )


def attention_kernel(
    heads, tile, q_ref, k_ref, v_ref, g_ref, gt_ref, bias_ref, live_ref,
    o_ref, grads_ref, kt_ref, vt_ref, dk_ref, dv_ref,
):
    count_rows = k_ref.shape[0]
    head = pl.program_id(0)

    @pl.when(head == 0)
    def _():
        kt_ref[...] = k_ref[...].T
        vt_ref[...] = v_ref[...].T
        dk_ref[...] = jnp.zeros_like(dk_ref)
        dv_ref[...] = jnp.zeros_like(dv_ref)

    for first in range(0, count_rows, tile):
        seen = first + tile
        rows = pl.ds(first, tile)
        q = q_ref[rows, :]
        g = g_ref[rows, :]
        gt = gt_ref[:, rows]
        scores = dot(k_ref[:seen, :], q, 1, 1) + bias_ref[:seen, rows]
        peak = jnp.max(scores, axis=0, keepdims=True)
        weights = jnp.exp2((scores - peak) * (FACTOR * LOG2E))
        probs = weights * (1.0 / jnp.sum(weights, axis=0, keepdims=True))
        probs_low = probs.astype(jnp.bfloat16)
        out = dot(vt_ref[:, :seen], probs_low, 1, 0)
        out = (out * live_ref[:, rows]).astype(jnp.bfloat16)
        o_ref[rows, :] = out.T
        center = jnp.sum(
            gt.astype(jnp.float32) * out.astype(jnp.float32), axis=0, keepdims=True
        )
        grad_probs = dot(v_ref[:seen, :], gt, 1, 0)
        grad_scores = (probs * (grad_probs - center)).astype(jnp.bfloat16)
        grad_q = dot(kt_ref[:, :seen], grad_scores, 1, 0) * FACTOR
        columns = pl.ds(pl.multiple_of(head * HEAD, HEAD), HEAD)
        grads_ref[rows, columns] = grad_q.astype(jnp.bfloat16).T
        dk_ref[:seen, :] += dot(grad_scores, q, 1, 0)
        dv_ref[:seen, :] += dot(probs_low, g, 1, 0)

    @pl.when(head == heads - 1)
    def _():
        grads_ref[:, heads * HEAD : (heads + 1) * HEAD] = (dk_ref[...] * FACTOR).astype(
            jnp.bfloat16
        )
        grads_ref[:, (heads + 1) * HEAD :] = dv_ref[...].astype(jnp.bfloat16)


def attend(rows, grad, grad_t, bias, live, tile):
    count_rows, width = rows.shape
    heads = width // HEAD - 2
    block = lambda index: pl.BlockSpec((count_rows, HEAD), index)
    return pl.pallas_call(
        functools.partial(attention_kernel, heads, tile),
        grid=(heads,),
        in_specs=[
            block(lambda h: (0, h)),
            block(lambda h: (0, heads)),
            block(lambda h: (0, heads + 1)),
            block(lambda h: (0, h)),
            pl.BlockSpec((HEAD, count_rows), lambda h: (h, 0)),
            pl.BlockSpec((count_rows, count_rows), lambda h: (0, 0)),
            pl.BlockSpec((1, count_rows), lambda h: (0, 0)),
        ],
        out_specs=[
            block(lambda h: (0, h)),
            pl.BlockSpec((count_rows, width), lambda h: (0, 0)),
        ],
        out_shape=[
            jax.ShapeDtypeStruct((count_rows, heads * HEAD), jnp.bfloat16),
            jax.ShapeDtypeStruct((count_rows, width), jnp.bfloat16),
        ],
        scratch_shapes=[
            pltpu.VMEM((HEAD, count_rows), jnp.bfloat16),
            pltpu.VMEM((HEAD, count_rows), jnp.bfloat16),
            pltpu.VMEM((count_rows, HEAD), jnp.float32),
            pltpu.VMEM((count_rows, HEAD), jnp.float32),
        ],
        compiler_params=pltpu.CompilerParams(vmem_limit_bytes=24 * 2**20),
        cost_estimate=pl.CostEstimate(
            flops=12 * heads * count_rows * count_rows * HEAD,
            bytes_accessed=8 * 2**20,
            transcendentals=heads * count_rows * count_rows,
        ),
        name="attention",
    )(rows, rows, rows, grad, grad_t, bias, live)


def to_partner(packet, xor_value):
    groups = lax.axis_size("dp")

    def by(distance):
        route = [(group, group ^ distance) for group in range(groups)]
        return lambda block: lax.ppermute(block, "dp", route)

    return lax.switch(xor_value - 1, [by(distance) for distance in range(1, groups)], packet)


def on_device(
    queries, key_rows, value_rows_initial, grad_out, seg_ids, pair_mask, sender, moved_seq
):
    count_rows = grad_out.shape[0]
    shards = lax.axis_size("tensor")
    local = queries.shape[0]
    split = lambda block: block.reshape(local, shards, block.shape[1] // shards)
    outgoing = jnp.concatenate(
        [split(queries), split(key_rows), split(value_rows_initial)], axis=2
    ).transpose(1, 0, 2)
    width = outgoing.shape[2]
    query_width = grad_out.shape[1]
    rows = lax.all_to_all(outgoing, "tensor", split_axis=0, concat_axis=0, tiled=True)
    rows = rows.reshape(count_rows, width)

    group = lax.axis_index("dp")
    xor_value = pair_mask[0]
    partner = jnp.bitwise_xor(group, xor_value)
    own = seg_ids[group]
    theirs = seg_ids[partner]
    giving = sender[group] == 1
    moved_label = moved_seq[group]
    live = jnp.sum((own < SEQS).astype(jnp.int32))
    start = jnp.sum((own < moved_label).astype(jnp.int32))
    count = jnp.sum((theirs == moved_seq[partner]).astype(jnp.int32))
    positions = jnp.arange(count_rows, dtype=jnp.int32)
    slots = jnp.arange(MOVE, dtype=jnp.int32)
    is_live = own != SEQS
    is_moved = giving & (own == moved_label)
    keep = is_live & ~is_moved

    packet = to_partner(lax.dynamic_slice_in_dim(grad_out, live, MOVE, 0), xor_value)
    place = (is_moved[:, None] & (positions[:, None] - start == slots[None, :])).astype(
        jnp.bfloat16
    )
    grad = jnp.where(
        keep[:, None], grad_out, dot(place, packet, 1, 0).astype(jnp.bfloat16)
    )
    grad_t = grad.T
    allowed = (
        (own[:, None] == own[None, :])
        & is_live[None, :]
        & (positions[:, None] <= positions[None, :])
    ) | (positions[:, None] == positions[None, :])
    bias = jnp.where(allowed, jnp.float32(0), jnp.float32(BLOCKED))
    attention, grads = attend(
        rows, grad, grad_t, bias, is_live.astype(jnp.float32)[None, :], count_rows
    )
    restored = lax.all_to_all(
        grads.reshape(shards, local, width), "tensor", split_axis=0, concat_axis=0, tiled=True
    )
    returning = to_partner(dot(place, attention, 0, 0).astype(jnp.bfloat16), xor_value)
    arrive = (
        ~giving
        & (positions[:, None] - live == slots[None, :])
        & (slots[None, :] < count)
    ).astype(jnp.bfloat16)
    attention = jnp.where(
        keep[:, None], attention, dot(arrive, returning, 1, 0).astype(jnp.bfloat16)
    )
    restored = restored.transpose(1, 0, 2)
    head_width = width - query_width
    joined = lambda block: block.reshape(local, -1)
    return (
        attention,
        joined(restored[:, :, :query_width]),
        joined(restored[:, :, query_width : query_width + head_width // 2]),
        joined(restored[:, :, query_width + head_width // 2 :]),
    )


def solution(mesh):
    rows = P(("dp", "tensor"), None)
    heads = P("dp", "tensor")
    return jax.shard_map(
        on_device,
        mesh=mesh,
        in_specs=(rows, rows, rows, heads, P(), P(), P(), P()),
        out_specs=(heads, rows, rows, rows),
        check_vma=False,
    )
```

```python
import functools

import jax
import jax.numpy as jnp
from jax import lax
from jax.experimental import pallas as pl
from jax.experimental.pallas import tpu as pltpu
from jax.sharding import PartitionSpec as P

HEAD = 128
SEQS = 8
MOVE = 128
FACTOR = HEAD**-0.5
LOG2E = 1.4426950408889634
BLOCKED = -1e30
TILE = 128
TOGETHER = 4
F32 = jnp.float32
BF16 = jnp.bfloat16
VMEM = pl.BlockSpec(memory_space=pltpu.VMEM)
SMEM = pl.BlockSpec(memory_space=pltpu.SMEM)
HBM = pl.BlockSpec(memory_space=pltpu.HBM)


def dot(a, b, contract_a, contract_b):
    return lax.dot_general(
        a, b, (((contract_a,), (contract_b,)), ((), ())), preferred_element_type=F32
    )


def params(mebibytes):
    return pltpu.CompilerParams(vmem_limit_bytes=mebibytes * 2**20)


def cost(flops, moved):
    return pl.CostEstimate(flops=flops, bytes_accessed=moved, transcendentals=0)


def slots(parts, shards):
    first = 0
    for part in parts:
        width = part.shape[1] // shards
        yield part, width, first
        first += width


def pack_kernel(q_ref, k_ref, v_ref, packed_ref, block_ref, in_sems, out_sems):
    shards = packed_ref.shape[0]
    arriving = []
    for shard in range(shards):
        for index, (part, width, first) in enumerate(slots((q_ref, k_ref, v_ref), shards)):
            copy = pltpu.make_async_copy(
                part.at[:, shard * width : (shard + 1) * width],
                block_ref.at[shard, :, first : first + width],
                in_sems.at[shard, index],
            )
            copy.start()
            arriving.append(copy)
    leaving = []
    for shard in range(shards):
        for copy in arriving[3 * shard : 3 * shard + 3]:
            copy.wait()
        copy = pltpu.make_async_copy(
            block_ref.at[shard], packed_ref.at[shard], out_sems.at[shard]
        )
        copy.start()
        leaving.append(copy)
    for copy in leaving:
        copy.wait()


def pack(queries, key_rows, value_rows, shards):
    local = queries.shape[0]
    width = (queries.shape[1] + key_rows.shape[1] + value_rows.shape[1]) // shards
    return pl.pallas_call(
        pack_kernel,
        in_specs=[HBM] * 3,
        out_specs=HBM,
        out_shape=jax.ShapeDtypeStruct((shards, local, width), BF16),
        scratch_shapes=[
            pltpu.VMEM((shards, local, width), BF16),
            pltpu.SemaphoreType.DMA((shards, 3)),
            pltpu.SemaphoreType.DMA((shards,)),
        ],
        compiler_params=params(56),
        cost_estimate=cost(0, 4 * local * width * shards),
        name="pack_rows",
    )(queries, key_rows, value_rows)


def unpack_kernel(packed_ref, q_ref, k_ref, v_ref, sems):
    shards = packed_ref.shape[0]
    leaving = []
    for shard in range(shards):
        for index, (part, width, first) in enumerate(slots((q_ref, k_ref, v_ref), shards)):
            copy = pltpu.make_async_copy(
                packed_ref.at[shard, :, first : first + width],
                part.at[:, shard * width : (shard + 1) * width],
                sems.at[shard, index],
            )
            copy.start()
            leaving.append(copy)
    for copy in leaving:
        copy.wait()


def unpack(packed, query_width, head_width):
    shards, local, _ = packed.shape
    shape = lambda width: jax.ShapeDtypeStruct((local, shards * width), BF16)
    return pl.pallas_call(
        unpack_kernel,
        in_specs=[VMEM],
        out_specs=[HBM] * 3,
        out_shape=[shape(query_width), shape(head_width), shape(head_width)],
        scratch_shapes=[pltpu.SemaphoreType.DMA((shards, 3))],
        compiler_params=params(8),
        cost_estimate=cost(0, 4 * packed.size),
        name="unpack_rows",
    )(packed)


def one_hot(hits):
    return hits.astype(F32).astype(BF16)


def iota(shape, dimension):
    return lax.broadcasted_iota(jnp.int32, shape, dimension)


def layout_kernel(
    group_ref, mask_ref, sender_ref, moved_ref, seg_ref, grad_ref, packet_ref, facts_ref, live_ref
):
    count = seg_ref.shape[1]
    group = group_ref[0]
    partner = jnp.bitwise_xor(group, mask_ref[0])
    giving = sender_ref[group] == 1
    own = seg_ref[pl.ds(group, 1), :]
    theirs = seg_ref[pl.ds(partner, 1), :]
    moved = jnp.where(giving, moved_ref[group], -1)
    number = lambda hits: jnp.sum(hits.astype(F32), axis=1, keepdims=True).astype(jnp.int32)
    live = number(own < SEQS)
    start = number(own < moved)
    handed = jnp.where(giving, 0, number(theirs == moved_ref[partner]))
    wide = lambda value: jnp.broadcast_to(value, (1, count))
    facts_ref[0:1, :] = own
    facts_ref[1:2, :] = jnp.full((1, count), moved, jnp.int32)
    facts_ref[2:3, :] = wide(start)
    facts_ref[3:4, :] = wide(live)
    facts_ref[4:5, :] = wide(handed)
    facts_ref[5:8, :] = jnp.zeros((3, count), jnp.int32)
    live_ref[0] = jnp.sum((own < SEQS).astype(F32)).astype(jnp.int32)
    take = one_hot(iota((MOVE, count), 1) - live == iota((MOVE, count), 0))
    packet_ref[...] = dot(take, grad_ref[...], 1, 0).astype(BF16)


def layout(group, pair_mask, sender, moved_seq, seg_ids, grad_out):
    count, width = grad_out.shape
    return pl.pallas_call(
        layout_kernel,
        in_specs=[SMEM] * 4 + [VMEM] * 2,
        out_specs=[VMEM, VMEM, SMEM],
        out_shape=[
            jax.ShapeDtypeStruct((MOVE, width), BF16),
            jax.ShapeDtypeStruct((8, count), jnp.int32),
            jax.ShapeDtypeStruct((1,), jnp.int32),
        ],
        compiler_params=params(8),
        cost_estimate=cost(2 * MOVE * count * width, 2**20),
        name="layout",
    )(group, pair_mask, sender, moved_seq, seg_ids, grad_out)


def finish_kernel(live_ref, facts_ref, packet_ref, out_ref, final_ref, window_ref, sem):
    del out_ref
    count = final_ref.shape[0]
    size = window_ref.shape[0]
    base = pl.multiple_of(jnp.minimum(live_ref[0] // 16 * 16, count - size), 16)
    rows = final_ref.at[pl.ds(base, size), :]
    fetch = pltpu.make_async_copy(rows, window_ref, sem.at[0])
    fetch.start()
    fetch.wait()
    row = iota((size, MOVE), 0) + base
    slot = iota((size, MOVE), 1)
    arrive = one_hot((row - facts_ref[3:4, :MOVE] == slot) & (slot < facts_ref[4:5, :MOVE]))
    window_ref[...] += dot(arrive, packet_ref[...], 1, 0).astype(BF16)
    store = pltpu.make_async_copy(window_ref, rows, sem.at[1])
    store.start()
    store.wait()


def finish(live, facts, packet, attention):
    return pl.pallas_call(
        finish_kernel,
        in_specs=[SMEM, VMEM, VMEM, HBM],
        out_specs=HBM,
        out_shape=jax.ShapeDtypeStruct(attention.shape, BF16),
        scratch_shapes=[
            pltpu.VMEM((MOVE + 16, attention.shape[1]), BF16),
            pltpu.SemaphoreType.DMA((2,)),
        ],
        input_output_aliases={3: 0},
        compiler_params=params(8),
        cost_estimate=cost(2 * MOVE * MOVE * attention.shape[1], 2**20),
        name="finish_out",
    )(live, facts, packet, attention)


def attention_kernel(
    x_ref, facts_ref, packet_hbm, grad_hbm,
    final_hbm, returning_ref, grads_hbm,
    packet_ref, g_ref, gt_ref, bias_ref, keep_ref, place_ref,
    kt_ref, vt_ref, dk_ref, dv_ref, o_ref, out_ref, in_sems, out_sems,
):
    count, width = x_ref.shape
    heads = width // HEAD - 2
    steps = heads // TOGETHER
    block = lambda step: slice(step * TOGETHER * HEAD, (step + 1) * TOGETHER * HEAD)
    fetches = [pltpu.make_async_copy(packet_hbm, packet_ref, in_sems.at[steps])] + [
        pltpu.make_async_copy(
            grad_hbm.at[:, block(step)], g_ref.at[:, block(step)], in_sems.at[step]
        )
        for step in range(steps)
    ]
    for fetch in fetches:
        fetch.start()

    own = facts_ref[0:1, :]
    moved, start = facts_ref[1:2, :MOVE], facts_ref[2:3, :MOVE]
    live = (own < SEQS).astype(F32)
    own_column = jnp.broadcast_to(own.astype(F32), (MOVE, count)).T.astype(jnp.int32)
    row, slot = iota((count, MOVE), 0), iota((count, MOVE), 1)
    keep_ref[...] = one_hot((own_column < SEQS) & (own_column != moved))
    place_ref[...] = one_hot((own_column == moved) & (row - start == slot))
    place_t = one_hot(
        (own == facts_ref[1:2, :]) & (iota((MOVE, count), 1) - facts_ref[2:3, :] == iota((MOVE, count), 0))
    )
    for first in range(0, count, MOVE):
        columns = slice(first, first + MOVE)
        seen = first + MOVE
        u, t = row[:seen], slot[:seen] + first
        theirs = own_column[:seen]
        allowed = ((theirs == own[:, columns]) & (theirs < SEQS) & (u <= t)) | (u == t)
        bias_ref[:seen, columns] = jnp.where(allowed, F32(0), F32(BLOCKED))
    k_ref = x_ref.at[:, heads * HEAD : (heads + 1) * HEAD]
    v_ref = x_ref.at[:, (heads + 1) * HEAD :]
    kt_ref[...] = k_ref[...].T
    vt_ref[...] = v_ref[...].T
    dk_ref[...] = jnp.zeros_like(dk_ref)
    dv_ref[...] = jnp.zeros_like(dv_ref)

    def send(source, target, columns, index):
        return pltpu.make_async_copy(
            source.at[:, columns], target.at[:, columns], out_sems.at[index]
        )

    leaving = []
    for step in range(steps):
        columns = block(step)
        here = [
            slice(head * HEAD, (head + 1) * HEAD)
            for head in range(step * TOGETHER, (step + 1) * TOGETHER)
        ]
        work = [
            (head, slice(first, first + TILE), first + TILE)
            for first in range(0, count, TILE)
            for head in here
        ]
        scores, grad_probs, probs, outs = [], [], [], []
        for head, rows, seen in work:
            scores.append(dot(k_ref[:seen, :], x_ref[rows, head], 1, 1) + bias_ref[:seen, rows])
        if step == 0:
            fetches[0].wait()
        fetches[1 + step].wait()
        for head in here:
            placed = dot(place_ref[...], packet_ref[:, head], 1, 0).astype(BF16)
            merged = g_ref[:, head] * keep_ref[...] + placed
            g_ref[:, head] = merged
            gt_ref[head, :] = merged.T
        for head, rows, seen in work:
            grad_probs.append(dot(v_ref[:seen, :], gt_ref[head, rows], 1, 0))
        for (head, rows, seen), score in zip(work, scores):
            peak = jnp.max(score, axis=0, keepdims=True)
            weights = jnp.exp2((score - peak) * (FACTOR * LOG2E))
            prob = weights * (1.0 / jnp.sum(weights, axis=0, keepdims=True))
            low = prob.astype(BF16)
            out = dot(vt_ref[:, :seen], low, 1, 0)
            out = (out * live[:, rows]).astype(BF16)
            o_ref[rows, head] = out.T
            dv_ref[:seen, :] += dot(low, g_ref[rows, head], 1, 0)
            probs.append(prob)
            outs.append(out)
        for (head, rows, seen), prob, grad_prob, out in zip(work, probs, grad_probs, outs):
            center = jnp.sum(
                gt_ref[head, rows].astype(F32) * out.astype(F32), axis=0, keepdims=True
            )
            grad_score = (prob * (grad_prob - center)).astype(BF16)
            grad_q = dot(kt_ref[:, :seen], grad_score, 1, 0) * FACTOR
            out_ref[rows, head] = grad_q.astype(BF16).T
            dk_ref[:seen, :] += dot(grad_score, x_ref[rows, head], 1, 0)
        leaving.append(send(out_ref, grads_hbm, columns, 2 * step))
        leaving[-1].start()
        returning_ref[:, columns] = dot(place_t, o_ref[:, columns], 1, 0).astype(BF16)
        for head in here:
            o_ref[:, head] = o_ref[:, head] * keep_ref[...]
        leaving.append(send(o_ref, final_hbm, columns, 2 * step + 1))
        leaving[-1].start()
    out_ref[:, heads * HEAD : (heads + 1) * HEAD] = (dk_ref[...] * FACTOR).astype(BF16)
    out_ref[:, (heads + 1) * HEAD :] = dv_ref[...].astype(BF16)
    leaving.append(send(out_ref, grads_hbm, slice(heads * HEAD, width), 2 * steps))
    leaving[-1].start()
    for copy in leaving:
        copy.wait()


def attend(rows, facts, packet, grad):
    count, width = rows.shape
    heads = width // HEAD - 2
    steps = heads // TOGETHER
    return pl.pallas_call(
        attention_kernel,
        in_specs=[VMEM, VMEM, HBM, HBM],
        out_specs=[HBM, VMEM, HBM],
        out_shape=[
            jax.ShapeDtypeStruct((count, heads * HEAD), BF16),
            jax.ShapeDtypeStruct((MOVE, heads * HEAD), BF16),
            jax.ShapeDtypeStruct((count, width), BF16),
        ],
        scratch_shapes=[
            pltpu.VMEM((MOVE, heads * HEAD), BF16),
            pltpu.VMEM((count, heads * HEAD), BF16),
            pltpu.VMEM((heads * HEAD, count), BF16),
            pltpu.VMEM((count, count), F32),
            pltpu.VMEM((count, MOVE), BF16),
            pltpu.VMEM((count, MOVE), BF16),
            pltpu.VMEM((HEAD, count), BF16),
            pltpu.VMEM((HEAD, count), BF16),
            pltpu.VMEM((count, HEAD), F32),
            pltpu.VMEM((count, HEAD), F32),
            pltpu.VMEM((count, heads * HEAD), BF16),
            pltpu.VMEM((count, width), BF16),
            pltpu.SemaphoreType.DMA((steps + 1,)),
            pltpu.SemaphoreType.DMA((2 * steps + 1,)),
        ],
        compiler_params=params(48),
        cost_estimate=cost(12 * heads * count * count * HEAD, 8 * 2**20),
        name="attention",
    )(rows, facts, packet, grad)


def to_partner(packet, xor_value):
    groups = lax.axis_size("dp")

    def by(distance):
        route = [(group, group ^ distance) for group in range(groups)]
        return lambda block: lax.ppermute(block, "dp", route)

    return lax.switch(xor_value - 1, [by(distance) for distance in range(1, groups)], packet)


def on_device(
    queries, key_rows, value_rows_initial, grad_out, seg_ids, pair_mask, sender, moved_seq
):
    count, query_width = grad_out.shape
    shards = lax.axis_size("tensor")
    outgoing = pack(queries, key_rows, value_rows_initial, shards)
    rows = lax.all_to_all(outgoing, "tensor", split_axis=0, concat_axis=0, tiled=True)
    width = rows.shape[2]

    group = lax.axis_index("dp").reshape(1)
    packet, facts, live = layout(group, pair_mask, sender, moved_seq, seg_ids, grad_out)
    packet = to_partner(packet, pair_mask[0])
    attention, returning, grads = attend(rows.reshape(count, width), facts, packet, grad_out)
    restored = lax.all_to_all(
        grads.reshape(outgoing.shape), "tensor", split_axis=0, concat_axis=0, tiled=True
    )
    returning = to_partner(returning, pair_mask[0])
    attention = finish(live, facts, returning, attention)
    return (attention, *unpack(restored, query_width, (width - query_width) // 2))


def solution(mesh):
    rows = P(("dp", "tensor"), None)
    heads = P("dp", "tensor")
    return jax.shard_map(
        on_device,
        mesh=mesh,
        in_specs=(rows, rows, rows, heads, P(), P(), P(), P()),
        out_specs=(heads, rows, rows, rows),
        check_vma=False,
    )
```

```python
import functools

import jax
import jax.numpy as jnp
from jax import lax
from jax.experimental import pallas as pl
from jax.experimental.pallas import tpu as pltpu
from jax.sharding import PartitionSpec as P

HEAD = 128
SEQS = 8
MOVE = 128
FACTOR = HEAD**-0.5
LOG2E = 1.4426950408889634
BLOCKED = -1e30
TILE = 128
TOGETHER = 4
F32 = jnp.float32
BF16 = jnp.bfloat16
VMEM = pl.BlockSpec(memory_space=pltpu.VMEM)
SMEM = pl.BlockSpec(memory_space=pltpu.SMEM)
HBM = pl.BlockSpec(memory_space=pltpu.HBM)


def dot(a, b, contract_a, contract_b):
    return lax.dot_general(
        a, b, (((contract_a,), (contract_b,)), ((), ())), preferred_element_type=F32
    )


def params(mebibytes):
    return pltpu.CompilerParams(vmem_limit_bytes=mebibytes * 2**20)


def cost(flops, moved):
    return pl.CostEstimate(flops=flops, bytes_accessed=moved, transcendentals=0)


def slots(parts, shards):
    first = 0
    for part in parts:
        width = part.shape[1] // shards
        yield part, width, first
        first += width


def pack_kernel(q_ref, k_ref, v_ref, packed_ref, block_ref, in_sems, out_sems):
    shards = packed_ref.shape[0]
    arriving = []
    for shard in range(shards):
        for index, (part, width, first) in enumerate(slots((q_ref, k_ref, v_ref), shards)):
            copy = pltpu.make_async_copy(
                part.at[:, shard * width : (shard + 1) * width],
                block_ref.at[shard, :, first : first + width],
                in_sems.at[shard, index],
            )
            copy.start()
            arriving.append(copy)
    leaving = []
    for shard in range(shards):
        for copy in arriving[3 * shard : 3 * shard + 3]:
            copy.wait()
        copy = pltpu.make_async_copy(
            block_ref.at[shard], packed_ref.at[shard], out_sems.at[shard]
        )
        copy.start()
        leaving.append(copy)
    for copy in leaving:
        copy.wait()


def pack(queries, key_rows, value_rows, shards):
    local = queries.shape[0]
    width = (queries.shape[1] + key_rows.shape[1] + value_rows.shape[1]) // shards
    return pl.pallas_call(
        pack_kernel,
        in_specs=[HBM] * 3,
        out_specs=HBM,
        out_shape=jax.ShapeDtypeStruct((shards, local, width), BF16),
        scratch_shapes=[
            pltpu.VMEM((shards, local, width), BF16),
            pltpu.SemaphoreType.DMA((shards, 3)),
            pltpu.SemaphoreType.DMA((shards,)),
        ],
        compiler_params=params(56),
        cost_estimate=cost(0, 4 * local * width * shards),
        name="pack_rows",
    )(queries, key_rows, value_rows)


def unpack_kernel(packed_ref, q_ref, k_ref, v_ref, sems):
    shards = packed_ref.shape[0]
    leaving = []
    for shard in range(shards):
        for index, (part, width, first) in enumerate(slots((q_ref, k_ref, v_ref), shards)):
            copy = pltpu.make_async_copy(
                packed_ref.at[shard, :, first : first + width],
                part.at[:, shard * width : (shard + 1) * width],
                sems.at[shard, index],
            )
            copy.start()
            leaving.append(copy)
    for copy in leaving:
        copy.wait()


def unpack(packed, query_width, head_width):
    shards, local, _ = packed.shape
    shape = lambda width: jax.ShapeDtypeStruct((local, shards * width), BF16)
    return pl.pallas_call(
        unpack_kernel,
        in_specs=[VMEM],
        out_specs=[HBM] * 3,
        out_shape=[shape(query_width), shape(head_width), shape(head_width)],
        scratch_shapes=[pltpu.SemaphoreType.DMA((shards, 3))],
        compiler_params=params(8),
        cost_estimate=cost(0, 4 * packed.size),
        name="unpack_rows",
    )(packed)


def one_hot(hits):
    return hits.astype(F32).astype(BF16)


def iota(shape, dimension):
    return lax.broadcasted_iota(jnp.int32, shape, dimension)


def layout_kernel(
    group_ref, mask_ref, sender_ref, moved_ref, seg_ref, grad_ref, packet_ref, facts_ref, live_ref
):
    count = seg_ref.shape[1]
    group = group_ref[0]
    partner = jnp.bitwise_xor(group, mask_ref[0])
    giving = sender_ref[group] == 1
    own = seg_ref[pl.ds(group, 1), :]
    theirs = seg_ref[pl.ds(partner, 1), :]
    moved = jnp.where(giving, moved_ref[group], -1)
    number = lambda hits: jnp.sum(hits.astype(F32), axis=1, keepdims=True).astype(jnp.int32)
    live = number(own < SEQS)
    start = number(own < moved)
    handed = jnp.where(giving, 0, number(theirs == moved_ref[partner]))
    wide = lambda value: jnp.broadcast_to(value, (1, count))
    facts_ref[0:1, :] = own
    facts_ref[1:2, :] = jnp.full((1, count), moved, jnp.int32)
    facts_ref[2:3, :] = wide(start)
    facts_ref[3:4, :] = wide(live)
    facts_ref[4:5, :] = wide(handed)
    facts_ref[5:8, :] = jnp.zeros((3, count), jnp.int32)
    live_ref[0] = jnp.sum((own < SEQS).astype(F32)).astype(jnp.int32)
    take = one_hot(iota((MOVE, count), 1) - live == iota((MOVE, count), 0))
    packet_ref[...] = dot(take, grad_ref[...], 1, 0).astype(BF16)


def layout(group, pair_mask, sender, moved_seq, seg_ids, grad_out):
    count, width = grad_out.shape
    return pl.pallas_call(
        layout_kernel,
        in_specs=[SMEM] * 4 + [VMEM] * 2,
        out_specs=[VMEM, VMEM, SMEM],
        out_shape=[
            jax.ShapeDtypeStruct((MOVE, width), BF16),
            jax.ShapeDtypeStruct((8, count), jnp.int32),
            jax.ShapeDtypeStruct((1,), jnp.int32),
        ],
        compiler_params=params(8),
        cost_estimate=cost(2 * MOVE * count * width, 2**20),
        name="layout",
    )(group, pair_mask, sender, moved_seq, seg_ids, grad_out)


def finish_kernel(live_ref, facts_ref, packet_ref, out_ref, final_ref, window_ref, sem):
    del out_ref
    size = window_ref.shape[0]
    base = pl.multiple_of(
        jnp.minimum(live_ref[0] // 16 * 16, final_ref.shape[0] - size), 16
    )
    rows = final_ref.at[pl.ds(base, size), :]
    fetch = pltpu.make_async_copy(rows, window_ref, sem.at[0])
    fetch.start()
    slot = iota((size, MOVE), 1)
    arrive = one_hot(
        (iota((size, MOVE), 0) + base - facts_ref[3:4, :MOVE] == slot)
        & (slot < facts_ref[4:5, :MOVE])
    )
    placed = dot(arrive, packet_ref[...], 1, 0).astype(BF16)
    fetch.wait()
    window_ref[...] += placed
    store = pltpu.make_async_copy(window_ref, rows, sem.at[1])
    store.start()
    store.wait()


def finish(live, facts, packet, attention):
    return pl.pallas_call(
        finish_kernel,
        in_specs=[SMEM, VMEM, VMEM, HBM],
        out_specs=HBM,
        out_shape=jax.ShapeDtypeStruct(attention.shape, BF16),
        scratch_shapes=[
            pltpu.VMEM((MOVE + 16, attention.shape[1]), BF16),
            pltpu.SemaphoreType.DMA((2,)),
        ],
        input_output_aliases={3: 0},
        compiler_params=params(8),
        cost_estimate=cost(2 * MOVE * MOVE * attention.shape[1], 2**20),
        name="finish_out",
    )(live, facts, packet, attention)


def attention_kernel(
    x_ref, facts_ref, packet_hbm, grad_hbm,
    final_hbm, returning_ref, grads_hbm,
    packet_ref, g_ref, gt_ref, bias_ref, keep_ref, place_ref,
    kt_ref, vt_ref, dk_ref, dv_ref, o_ref, out_ref, in_sems, out_sems,
):
    count, width = x_ref.shape
    heads = width // HEAD - 2
    steps = heads // TOGETHER
    block = lambda step: slice(step * TOGETHER * HEAD, (step + 1) * TOGETHER * HEAD)
    fetches = [pltpu.make_async_copy(packet_hbm, packet_ref, in_sems.at[steps])] + [
        pltpu.make_async_copy(
            grad_hbm.at[:, block(step)], g_ref.at[:, block(step)], in_sems.at[step]
        )
        for step in range(steps)
    ]
    for fetch in fetches:
        fetch.start()

    own = facts_ref[0:1, :]
    moved, start = facts_ref[1:2, :MOVE], facts_ref[2:3, :MOVE]
    live = (own < SEQS).astype(F32)
    own_column = jnp.broadcast_to(own.astype(F32), (MOVE, count)).T.astype(jnp.int32)
    row, slot = iota((count, MOVE), 0), iota((count, MOVE), 1)
    keep_ref[...] = one_hot((own_column < SEQS) & (own_column != moved))
    place_ref[...] = one_hot((own_column == moved) & (row - start == slot))
    place_t = one_hot(
        (own == facts_ref[1:2, :]) & (iota((MOVE, count), 1) - facts_ref[2:3, :] == iota((MOVE, count), 0))
    )
    for first in range(0, count, MOVE):
        columns = slice(first, first + MOVE)
        seen = first + MOVE
        u, t = row[:seen], slot[:seen] + first
        theirs = own_column[:seen]
        allowed = ((theirs == own[:, columns]) & (theirs < SEQS) & (u <= t)) | (u == t)
        bias_ref[:seen, columns] = jnp.where(allowed, F32(0), F32(BLOCKED))
    k_ref = x_ref.at[:, heads * HEAD : (heads + 1) * HEAD]
    v_ref = x_ref.at[:, (heads + 1) * HEAD :]
    kt_ref[...] = k_ref[...].T
    vt_ref[...] = v_ref[...].T
    dk_ref[...] = jnp.zeros_like(dk_ref)
    dv_ref[...] = jnp.zeros_like(dv_ref)

    def send(source, target, columns, index):
        return pltpu.make_async_copy(
            source.at[:, columns], target.at[:, columns], out_sems.at[index]
        )

    everything = [slice(head * HEAD, (head + 1) * HEAD) for head in range(heads)]
    leaving = []
    for step in range(steps):
        columns = block(step)
        here = [
            slice(head * HEAD, (head + 1) * HEAD)
            for head in range(step * TOGETHER, (step + 1) * TOGETHER)
        ]
        tiles = [(slice(first, first + TILE), first + TILE) for first in range(0, count, TILE)]
        queries, scores, grad_probs, probs, outs = [], [], [], [], []
        for rows, seen in tiles:
            queries.append(jnp.concatenate([x_ref[rows, head] for head in here], axis=0))
            bias = jnp.concatenate([bias_ref[:seen, rows]] * TOGETHER, axis=1)
            scores.append(dot(k_ref[:seen, :], queries[-1], 1, 1) + bias)
        if step == 0:
            for fetch in fetches:
                fetch.wait()
        for head in everything if step == 0 else ():
            placed = dot(place_ref[...], packet_ref[:, head], 1, 0).astype(BF16)
            merged = g_ref[:, head] * keep_ref[...] + placed
            g_ref[:, head] = merged
            gt_ref[head, :] = merged.T
        for rows, seen in tiles:
            grad_t = jnp.concatenate([gt_ref[head, rows] for head in here], axis=1)
            grad_probs.append(dot(v_ref[:seen, :], grad_t, 1, 0))
        for (rows, seen), score in zip(tiles, scores):
            peak = jnp.max(score, axis=0, keepdims=True)
            weights = jnp.exp2((score - peak) * (FACTOR * LOG2E))
            prob = weights * (1.0 / jnp.sum(weights, axis=0, keepdims=True))
            low = prob.astype(BF16)
            out = dot(vt_ref[:, :seen], low, 1, 0)
            out = (out * jnp.concatenate([live[:, rows]] * TOGETHER, axis=1)).astype(BF16)
            for index, head in enumerate(here):
                o_ref[rows, head] = out[:, index * TILE : (index + 1) * TILE].T
            grad = jnp.concatenate([g_ref[rows, head] for head in here], axis=0)
            dv_ref[:seen, :] += dot(low, grad, 1, 0)
            probs.append(prob)
            outs.append(out)
        for (rows, seen), query, prob, grad_prob, out in zip(
            tiles, queries, probs, grad_probs, outs
        ):
            grad_t = jnp.concatenate([gt_ref[head, rows] for head in here], axis=1)
            center = jnp.sum(grad_t.astype(F32) * out.astype(F32), axis=0, keepdims=True)
            grad_score = (prob * (grad_prob - center)).astype(BF16)
            grad_q = (dot(kt_ref[:, :seen], grad_score, 1, 0) * FACTOR).astype(BF16)
            for index, head in enumerate(here):
                out_ref[rows, head] = grad_q[:, index * TILE : (index + 1) * TILE].T
            dk_ref[:seen, :] += dot(grad_score, query, 1, 0)
        leaving.append(send(out_ref, grads_hbm, columns, 2 * step))
        leaving[-1].start()
        returning_ref[:, columns] = dot(place_t, o_ref[:, columns], 1, 0).astype(BF16)
        for head in here:
            o_ref[:, head] = o_ref[:, head] * keep_ref[...]
        leaving.append(send(o_ref, final_hbm, columns, 2 * step + 1))
        leaving[-1].start()
    out_ref[:, heads * HEAD : (heads + 1) * HEAD] = (dk_ref[...] * FACTOR).astype(BF16)
    out_ref[:, (heads + 1) * HEAD :] = dv_ref[...].astype(BF16)
    leaving.append(send(out_ref, grads_hbm, slice(heads * HEAD, width), 2 * steps))
    leaving[-1].start()
    for copy in leaving:
        copy.wait()


def attend(rows, facts, packet, grad):
    count, width = rows.shape
    heads = width // HEAD - 2
    steps = heads // TOGETHER
    return pl.pallas_call(
        attention_kernel,
        in_specs=[VMEM, VMEM, HBM, HBM],
        out_specs=[HBM, VMEM, HBM],
        out_shape=[
            jax.ShapeDtypeStruct((count, heads * HEAD), BF16),
            jax.ShapeDtypeStruct((MOVE, heads * HEAD), BF16),
            jax.ShapeDtypeStruct((count, width), BF16),
        ],
        scratch_shapes=[
            pltpu.VMEM((MOVE, heads * HEAD), BF16),
            pltpu.VMEM((count, heads * HEAD), BF16),
            pltpu.VMEM((heads * HEAD, count), BF16),
            pltpu.VMEM((count, count), F32),
            pltpu.VMEM((count, MOVE), BF16),
            pltpu.VMEM((count, MOVE), BF16),
            pltpu.VMEM((HEAD, count), BF16),
            pltpu.VMEM((HEAD, count), BF16),
            pltpu.VMEM((count, HEAD), F32),
            pltpu.VMEM((count, HEAD), F32),
            pltpu.VMEM((count, heads * HEAD), BF16),
            pltpu.VMEM((count, width), BF16),
            pltpu.SemaphoreType.DMA((steps + 1,)),
            pltpu.SemaphoreType.DMA((2 * steps + 1,)),
        ],
        compiler_params=params(48),
        cost_estimate=cost(12 * heads * count * count * HEAD, 8 * 2**20),
        name="attention",
    )(rows, facts, packet, grad)


def to_partner(packet, xor_value):
    groups = lax.axis_size("dp")

    def by(distance):
        route = [(group, group ^ distance) for group in range(groups)]
        return lambda block: lax.ppermute(block, "dp", route)

    return lax.switch(xor_value - 1, [by(distance) for distance in range(1, groups)], packet)


def on_device(
    queries, key_rows, value_rows_initial, grad_out, seg_ids, pair_mask, sender, moved_seq
):
    count, query_width = grad_out.shape
    shards = lax.axis_size("tensor")
    outgoing = pack(queries, key_rows, value_rows_initial, shards)
    rows = lax.all_to_all(outgoing, "tensor", split_axis=0, concat_axis=0, tiled=True)
    width = rows.shape[2]

    group = lax.axis_index("dp").reshape(1)
    packet, facts, live = layout(group, pair_mask, sender, moved_seq, seg_ids, grad_out)
    packet = to_partner(packet, pair_mask[0])
    attention, returning, grads = attend(rows.reshape(count, width), facts, packet, grad_out)
    restored = lax.all_to_all(
        grads.reshape(outgoing.shape), "tensor", split_axis=0, concat_axis=0, tiled=True
    )
    returning = to_partner(returning, pair_mask[0])
    attention = finish(live, facts, returning, attention)
    return (attention, *unpack(restored, query_width, (width - query_width) // 2))


def solution(mesh):
    rows = P(("dp", "tensor"), None)
    heads = P("dp", "tensor")
    return jax.shard_map(
        on_device,
        mesh=mesh,
        in_specs=(rows, rows, rows, heads, P(), P(), P(), P()),
        out_specs=(heads, rows, rows, rows),
        check_vma=False,
    )
```

```python
import functools

import jax
import jax.numpy as jnp
from jax import lax
from jax.experimental import pallas as pl
from jax.experimental.pallas import tpu as pltpu
from jax.sharding import PartitionSpec as P

HEAD = 128
SEQS = 8
MOVE = 128
FACTOR = HEAD**-0.5
LOG2E = 1.4426950408889634
BLOCKED = -1e30
TILE = 128
TOGETHER = 4
F32 = jnp.float32
BF16 = jnp.bfloat16
VMEM = pl.BlockSpec(memory_space=pltpu.VMEM)
SMEM = pl.BlockSpec(memory_space=pltpu.SMEM)
HBM = pl.BlockSpec(memory_space=pltpu.HBM)


def dot(a, b, contract_a, contract_b):
    return lax.dot_general(
        a, b, (((contract_a,), (contract_b,)), ((), ())), preferred_element_type=F32
    )


def params(mebibytes):
    return pltpu.CompilerParams(vmem_limit_bytes=mebibytes * 2**20)


def cost(flops, moved):
    return pl.CostEstimate(flops=flops, bytes_accessed=moved, transcendentals=0)


def slots(parts, shards):
    first = 0
    for part in parts:
        width = part.shape[1] // shards
        yield part, width, first
        first += width


def pack_kernel(q_ref, k_ref, v_ref, packed_ref, block_ref, in_sems, out_sems):
    shards = packed_ref.shape[0]
    arriving = []
    for shard in range(shards):
        for index, (part, width, first) in enumerate(slots((q_ref, k_ref, v_ref), shards)):
            copy = pltpu.make_async_copy(
                part.at[:, shard * width : (shard + 1) * width],
                block_ref.at[shard, :, first : first + width],
                in_sems.at[shard, index],
            )
            copy.start()
            arriving.append(copy)
    leaving = []
    for shard in range(shards):
        for copy in arriving[3 * shard : 3 * shard + 3]:
            copy.wait()
        copy = pltpu.make_async_copy(
            block_ref.at[shard], packed_ref.at[shard], out_sems.at[shard]
        )
        copy.start()
        leaving.append(copy)
    for copy in leaving:
        copy.wait()


def pack(queries, key_rows, value_rows, shards):
    local = queries.shape[0]
    width = (queries.shape[1] + key_rows.shape[1] + value_rows.shape[1]) // shards
    return pl.pallas_call(
        pack_kernel,
        in_specs=[HBM] * 3,
        out_specs=HBM,
        out_shape=jax.ShapeDtypeStruct((shards, local, width), BF16),
        scratch_shapes=[
            pltpu.VMEM((shards, local, width), BF16),
            pltpu.SemaphoreType.DMA((shards, 3)),
            pltpu.SemaphoreType.DMA((shards,)),
        ],
        compiler_params=params(56),
        cost_estimate=cost(0, 4 * local * width * shards),
        name="pack_rows",
    )(queries, key_rows, value_rows)


def one_hot(hits):
    return hits.astype(F32).astype(BF16)


def iota(shape, dimension):
    return lax.broadcasted_iota(jnp.int32, shape, dimension)


def layout_kernel(
    group_ref, mask_ref, sender_ref, moved_ref, seg_ref, grad_ref, packet_ref, facts_ref, live_ref
):
    count = seg_ref.shape[1]
    group = group_ref[0]
    partner = jnp.bitwise_xor(group, mask_ref[0])
    giving = sender_ref[group] == 1
    own = seg_ref[pl.ds(group, 1), :]
    theirs = seg_ref[pl.ds(partner, 1), :]
    moved = jnp.where(giving, moved_ref[group], -1)
    number = lambda hits: jnp.sum(hits.astype(F32), axis=1, keepdims=True).astype(jnp.int32)
    live = number(own < SEQS)
    start = number(own < moved)
    handed = jnp.where(giving, 0, number(theirs == moved_ref[partner]))
    wide = lambda value: jnp.broadcast_to(value, (1, count))
    facts_ref[0:1, :] = own
    facts_ref[1:2, :] = jnp.full((1, count), moved, jnp.int32)
    facts_ref[2:3, :] = wide(start)
    facts_ref[3:4, :] = wide(live)
    facts_ref[4:5, :] = wide(handed)
    facts_ref[5:8, :] = jnp.zeros((3, count), jnp.int32)
    live_ref[0] = jnp.sum((own < SEQS).astype(F32)).astype(jnp.int32)
    take = one_hot(iota((MOVE, count), 1) - live == iota((MOVE, count), 0))
    packet_ref[...] = dot(take, grad_ref[...], 1, 0).astype(BF16)


def layout(group, pair_mask, sender, moved_seq, seg_ids, grad_out):
    count, width = grad_out.shape
    return pl.pallas_call(
        layout_kernel,
        in_specs=[SMEM] * 4 + [VMEM] * 2,
        out_specs=[VMEM, VMEM, SMEM],
        out_shape=[
            jax.ShapeDtypeStruct((MOVE, width), BF16),
            jax.ShapeDtypeStruct((8, count), jnp.int32),
            jax.ShapeDtypeStruct((1,), jnp.int32),
        ],
        compiler_params=params(8),
        cost_estimate=cost(2 * MOVE * count * width, 2**20),
        name="layout",
    )(group, pair_mask, sender, moved_seq, seg_ids, grad_out)


def finish_kernel(
    live_ref, facts_ref, packet_ref, packed_ref, out_ref,
    final_ref, q_ref, k_ref, v_ref, window_ref, sem, unpack_sems,
):
    del out_ref
    size = window_ref.shape[0]
    base = pl.multiple_of(
        jnp.minimum(live_ref[0] // 16 * 16, final_ref.shape[0] - size), 16
    )
    rows = final_ref.at[pl.ds(base, size), :]
    fetch = pltpu.make_async_copy(rows, window_ref, sem.at[0])
    fetch.start()
    shards = packed_ref.shape[0]
    leaving = []
    for shard in range(shards):
        for index, (part, width, first) in enumerate(slots((q_ref, k_ref, v_ref), shards)):
            copy = pltpu.make_async_copy(
                packed_ref.at[shard, :, first : first + width],
                part.at[:, shard * width : (shard + 1) * width],
                unpack_sems.at[shard, index],
            )
            copy.start()
            leaving.append(copy)
    slot = iota((size, MOVE), 1)
    arrive = one_hot(
        (iota((size, MOVE), 0) + base - facts_ref[3:4, :MOVE] == slot)
        & (slot < facts_ref[4:5, :MOVE])
    )
    placed = dot(arrive, packet_ref[...], 1, 0).astype(BF16)
    fetch.wait()
    window_ref[...] += placed
    store = pltpu.make_async_copy(window_ref, rows, sem.at[1])
    store.start()
    for copy in leaving:
        copy.wait()
    store.wait()


def finish(live, facts, packet, packed, attention, query_width, head_width):
    shards, local, _ = packed.shape
    shape = lambda width: jax.ShapeDtypeStruct((local, shards * width), BF16)
    return pl.pallas_call(
        finish_kernel,
        in_specs=[SMEM, VMEM, VMEM, VMEM, HBM],
        out_specs=[HBM] * 4,
        out_shape=[
            jax.ShapeDtypeStruct(attention.shape, BF16),
            shape(query_width),
            shape(head_width),
            shape(head_width),
        ],
        scratch_shapes=[
            pltpu.VMEM((MOVE + 16, attention.shape[1]), BF16),
            pltpu.SemaphoreType.DMA((2,)),
            pltpu.SemaphoreType.DMA((shards, 3)),
        ],
        input_output_aliases={4: 0},
        compiler_params=params(8),
        cost_estimate=cost(2 * MOVE * MOVE * attention.shape[1], 4 * packed.size),
        name="finish_rows",
    )(live, facts, packet, packed, attention)


def attention_kernel(
    x_ref, facts_ref, packet_hbm, grad_hbm,
    final_hbm, returning_ref, grads_hbm,
    packet_ref, g_ref, gt_ref, bias_ref, keep_ref, place_ref,
    kt_ref, vt_ref, dk_ref, dv_ref, o_ref, out_ref, in_sems, out_sems,
):
    count, width = x_ref.shape
    heads = width // HEAD - 2
    steps = heads // TOGETHER
    block = lambda step: slice(step * TOGETHER * HEAD, (step + 1) * TOGETHER * HEAD)
    fetches = [pltpu.make_async_copy(packet_hbm, packet_ref, in_sems.at[steps])] + [
        pltpu.make_async_copy(
            grad_hbm.at[:, block(step)], g_ref.at[:, block(step)], in_sems.at[step]
        )
        for step in range(steps)
    ]
    for fetch in fetches:
        fetch.start()

    own = facts_ref[0:1, :]
    moved, start = facts_ref[1:2, :MOVE], facts_ref[2:3, :MOVE]
    live = (own < SEQS).astype(F32)
    own_column = jnp.broadcast_to(own.astype(F32), (MOVE, count)).T.astype(jnp.int32)
    row, slot = iota((count, MOVE), 0), iota((count, MOVE), 1)
    keep_ref[...] = one_hot((own_column < SEQS) & (own_column != moved))
    place_ref[...] = one_hot((own_column == moved) & (row - start == slot))
    place_t = one_hot(
        (own == facts_ref[1:2, :]) & (iota((MOVE, count), 1) - facts_ref[2:3, :] == iota((MOVE, count), 0))
    )
    for first in range(0, count, MOVE):
        columns = slice(first, first + MOVE)
        seen = first + MOVE
        u, t = row[:seen], slot[:seen] + first
        theirs = own_column[:seen]
        allowed = ((theirs == own[:, columns]) & (theirs < SEQS) & (u <= t)) | (u == t)
        bias_ref[:seen, columns] = jnp.where(allowed, F32(0), F32(BLOCKED))
    k_ref = x_ref.at[:, heads * HEAD : (heads + 1) * HEAD]
    v_ref = x_ref.at[:, (heads + 1) * HEAD :]
    kt_ref[...] = k_ref[...].T
    vt_ref[...] = v_ref[...].T
    dk_ref[...] = jnp.zeros_like(dk_ref)
    dv_ref[...] = jnp.zeros_like(dv_ref)

    def send(source, target, columns, index):
        return pltpu.make_async_copy(
            source.at[:, columns], target.at[:, columns], out_sems.at[index]
        )

    everything = [slice(head * HEAD, (head + 1) * HEAD) for head in range(heads)]
    leaving = []
    for step in range(steps):
        columns = block(step)
        here = [
            slice(head * HEAD, (head + 1) * HEAD)
            for head in range(step * TOGETHER, (step + 1) * TOGETHER)
        ]
        tiles = [(slice(first, first + TILE), first + TILE) for first in range(0, count, TILE)]
        queries, scores, grad_probs, probs, outs = [], [], [], [], []
        for rows, seen in tiles:
            queries.append(jnp.concatenate([x_ref[rows, head] for head in here], axis=0))
            bias = jnp.concatenate([bias_ref[:seen, rows]] * TOGETHER, axis=1)
            scores.append(dot(k_ref[:seen, :], queries[-1], 1, 1) + bias)
        if step == 0:
            for fetch in fetches:
                fetch.wait()
        for head in everything if step == 0 else ():
            placed = dot(place_ref[...], packet_ref[:, head], 1, 0).astype(BF16)
            merged = g_ref[:, head] * keep_ref[...] + placed
            g_ref[:, head] = merged
            gt_ref[head, :] = merged.T
        for rows, seen in tiles:
            grad_t = jnp.concatenate([gt_ref[head, rows] for head in here], axis=1)
            grad_probs.append(dot(v_ref[:seen, :], grad_t, 1, 0))
        for (rows, seen), score in zip(tiles, scores):
            peak = jnp.max(score, axis=0, keepdims=True)
            weights = jnp.exp2((score - peak) * (FACTOR * LOG2E))
            prob = weights * (1.0 / jnp.sum(weights, axis=0, keepdims=True))
            low = prob.astype(BF16)
            out = dot(vt_ref[:, :seen], low, 1, 0)
            out = (out * jnp.concatenate([live[:, rows]] * TOGETHER, axis=1)).astype(BF16)
            for index, head in enumerate(here):
                o_ref[rows, head] = out[:, index * TILE : (index + 1) * TILE].T
            grad = jnp.concatenate([g_ref[rows, head] for head in here], axis=0)
            dv_ref[:seen, :] += dot(low, grad, 1, 0)
            probs.append(prob)
            outs.append(out)
        for (rows, seen), query, prob, grad_prob, out in zip(
            tiles, queries, probs, grad_probs, outs
        ):
            grad_t = jnp.concatenate([gt_ref[head, rows] for head in here], axis=1)
            center = jnp.sum(grad_t.astype(F32) * out.astype(F32), axis=0, keepdims=True)
            grad_score = (prob * (grad_prob - center)).astype(BF16)
            grad_q = (dot(kt_ref[:, :seen], grad_score, 1, 0) * FACTOR).astype(BF16)
            for index, head in enumerate(here):
                out_ref[rows, head] = grad_q[:, index * TILE : (index + 1) * TILE].T
            dk_ref[:seen, :] += dot(grad_score, query, 1, 0)
        leaving.append(send(out_ref, grads_hbm, columns, 2 * step))
        leaving[-1].start()
        returning_ref[:, columns] = dot(place_t, o_ref[:, columns], 1, 0).astype(BF16)
        for head in here:
            o_ref[:, head] = o_ref[:, head] * keep_ref[...]
        leaving.append(send(o_ref, final_hbm, columns, 2 * step + 1))
        leaving[-1].start()
    out_ref[:, heads * HEAD : (heads + 1) * HEAD] = (dk_ref[...] * FACTOR).astype(BF16)
    out_ref[:, (heads + 1) * HEAD :] = dv_ref[...].astype(BF16)
    leaving.append(send(out_ref, grads_hbm, slice(heads * HEAD, width), 2 * steps))
    leaving[-1].start()
    for copy in leaving:
        copy.wait()


def attend(rows, facts, packet, grad):
    count, width = rows.shape
    heads = width // HEAD - 2
    steps = heads // TOGETHER
    return pl.pallas_call(
        attention_kernel,
        in_specs=[VMEM, VMEM, HBM, HBM],
        out_specs=[HBM, VMEM, HBM],
        out_shape=[
            jax.ShapeDtypeStruct((count, heads * HEAD), BF16),
            jax.ShapeDtypeStruct((MOVE, heads * HEAD), BF16),
            jax.ShapeDtypeStruct((count, width), BF16),
        ],
        scratch_shapes=[
            pltpu.VMEM((MOVE, heads * HEAD), BF16),
            pltpu.VMEM((count, heads * HEAD), BF16),
            pltpu.VMEM((heads * HEAD, count), BF16),
            pltpu.VMEM((count, count), F32),
            pltpu.VMEM((count, MOVE), BF16),
            pltpu.VMEM((count, MOVE), BF16),
            pltpu.VMEM((HEAD, count), BF16),
            pltpu.VMEM((HEAD, count), BF16),
            pltpu.VMEM((count, HEAD), F32),
            pltpu.VMEM((count, HEAD), F32),
            pltpu.VMEM((count, heads * HEAD), BF16),
            pltpu.VMEM((count, width), BF16),
            pltpu.SemaphoreType.DMA((steps + 1,)),
            pltpu.SemaphoreType.DMA((2 * steps + 1,)),
        ],
        compiler_params=params(48),
        cost_estimate=cost(12 * heads * count * count * HEAD, 8 * 2**20),
        name="attention",
    )(rows, facts, packet, grad)


def to_partner(packet, xor_value):
    groups = lax.axis_size("dp")

    def by(distance):
        route = [(group, group ^ distance) for group in range(groups)]
        return lambda block: lax.ppermute(block, "dp", route)

    return lax.switch(xor_value - 1, [by(distance) for distance in range(1, groups)], packet)


def on_device(
    queries, key_rows, value_rows_initial, grad_out, seg_ids, pair_mask, sender, moved_seq
):
    count, query_width = grad_out.shape
    shards = lax.axis_size("tensor")
    outgoing = pack(queries, key_rows, value_rows_initial, shards)
    rows = lax.all_to_all(outgoing, "tensor", split_axis=0, concat_axis=0, tiled=True)
    width = rows.shape[2]

    group = lax.axis_index("dp").reshape(1)
    packet, facts, live = layout(group, pair_mask, sender, moved_seq, seg_ids, grad_out)
    packet = to_partner(packet, pair_mask[0])
    attention, returning, grads = attend(rows.reshape(count, width), facts, packet, grad_out)
    restored = lax.all_to_all(
        grads.reshape(outgoing.shape), "tensor", split_axis=0, concat_axis=0, tiled=True
    )
    returning = to_partner(returning, pair_mask[0])
    return finish(
        live, facts, returning, restored, attention, query_width, (width - query_width) // 2
    )


def solution(mesh):
    rows = P(("dp", "tensor"), None)
    heads = P("dp", "tensor")
    return jax.shard_map(
        on_device,
        mesh=mesh,
        in_specs=(rows, rows, rows, heads, P(), P(), P(), P()),
        out_specs=(heads, rows, rows, rows),
        check_vma=False,
    )
```
